32 devices in a mesh: expert: 16 (over z, x, core), tensor: 2 (over y).
Axes of the slice: x: 2, y: 2, z: 4, core: 2. Of those that a mesh axis runs over, the one named last changes fastest.
Arguments:
- tokens: bfloat16 [384, 4096], P('expert', 'tensor'), may hold values from -6 to 6
- grad_out: bfloat16 [384, 4096], P('expert', 'tensor'), may hold values from -6 to 6
- routing: int32 [384, 8], P('expert'), may hold values from 0 to 15, all different within a row; in each aligned block of 24 rows (0 to 23, 24 to 47, ...) at most 24 rows name the same one
- gates: float32 [384, 8], P('expert'), may hold values from 0.1 to 1
- w_in: bfloat16 [16, 4096, 2, 1536], P('expert', None, None, 'tensor'), may hold values from -0.09375 to 0.09375
- w_out: bfloat16 [16, 1536, 4096], P('expert', 'tensor'), may hold values from -0.15625 to 0.15625
Outputs:
- mixed: bfloat16 [384, 4096], P('expert', 'tensor')
- grad_tokens: bfloat16 [384, 4096], P('expert', 'tensor')
- grad_w_out: bfloat16 [16, 1536, 4096], P('expert', 'tensor')
The draws below stay inside these ranges and needn't reach their ends.
Inputs may be any that keep to these rules, and one draw needn't show every extreme that they name: `routing`: each row names 8 different experts. Within each group of 24 tokens (the tokens held by one position of the `expert` axis (one token group)) no expert is named by more than 24 tokens, and some group names some expert exactly 24 times.
All inputs are finite; a program needn't handle non-finite values.
Results may differ from the reference program's by a relative error of at most 0.015.
Values may be sent and summed in bfloat16 or wider, within the bound.
A program may use at most 128 MiB of HBM per device.

```python
import math
import jax
import jax.numpy as jnp
import numpy as np
from jax import lax

D = 4096
FF = 1536
TOPK = 8
TOK_GRP = 24
EXPERTS = 16
CAP = 24
TOKENS = 384
N_TENSOR = 2


def block_scale(stream_key, shape, split, smallest, largest):
    level, own = 1.0, jax.random.fold_in(stream_key, 6)
    for dim, parts in split:
        draws = jnp.exp(jax.random.uniform(jax.random.fold_in(own, dim), (parts,), jnp.float32, smallest / len(split), largest / len(split)))
        level = level * jnp.repeat(draws, shape[dim] // parts).reshape([-1 if axis == dim else 1 for axis in range(len(shape))])
    return level


def routed_block(rng, own, number, rows, number_of, top, reach, lean):
    sequence = jax.random.permutation(rng, number_of)
    heavy_load, usual = portions_of(number_of, rows * top, reach, lean, True), portions_of(number_of, rows * top, reach, lean, False)
    places = jnp.arange(number_of)

    def named(tallies, rotation):
        used = int((tallies > 0).sum())
        fixed = max(1, used // 4)
        passed = fixed + (places - fixed + rotation * (used - fixed)) % max(1, number_of - fixed)
        return jnp.zeros((number_of,), jnp.int32).at[sequence[jnp.where(places < fixed, places, passed)]].set(jnp.asarray(tallies, jnp.int32))

    tallies = jnp.where(number % 4 == 0, named(heavy_load, number // 4), named(usual, number - number // 4 - 1))
    mixed = jax.random.permutation(jax.random.fold_in(own, 3), number_of)
    giver, sink = mixed[0:number_of // 2 * 2:2], mixed[1:number_of // 2 * 2:2]
    room = jnp.minimum(tallies[giver] - 1, reach - tallies[sink]) // 2
    room = jnp.where((giver == sequence[0]) | (sink == sequence[0]) | (tallies[sink] == 0), 0, jnp.maximum(room, 0))
    passed = jax.random.randint(jax.random.fold_in(own, 4), (number_of // 2,), 0, 1 << 20) % (room + 1)
    tallies = tallies.at[giver].add(-passed).at[sink].add(passed)
    members = jnp.searchsorted(jnp.cumsum(tallies), jnp.arange(rows * top), side="right").astype(jnp.int32)
    grid = members.reshape(top, rows).T
    grid = grid[jax.random.permutation(jax.random.fold_in(own, 1), rows)]
    rotation = jax.random.randint(jax.random.fold_in(own, 2), (rows, 1), 0, top)
    return jnp.take_along_axis(grid, (jnp.arange(top)[None, :] + rotation) % top, axis=1)


def portions_of(number_of, total, bound, lean, full):
    weights = [(1 << 20) // math.isqrt(grade ** lean) + 1 for grade in range(1, number_of + 1)]
    largest = bound if full else min(bound, max(-(-total // number_of), total * weights[0] // sum(weights)))
    least = 1 if total - largest >= number_of - 1 else 0
    holding, surplus = [largest] + [least] * (number_of - 1), total - largest - least * (number_of - 1)
    while surplus > 0:
        candidates = [i for i in range(1, number_of) if holding[i] < largest] or [i for i in range(1, number_of) if holding[i] < bound]
        pool, left = sum([weights[i] for i in candidates]), surplus
        for i in candidates:
            addition = min(bound - holding[i], max(1, left * weights[i] // pool), surplus)
            holding[i] = holding[i] + addition
            surplus = surplus - addition
    return np.array(holding)


def normal_values(stream_key, extent, width, most, cuts=(), held_as=jnp.bfloat16):
    loudness = block_scale(stream_key, extent, cuts, -0.22, 0.18) if cuts else 1.0
    result = jax.random.normal(stream_key, extent, jnp.float32) * width * loudness
    return jnp.minimum(jnp.maximum(result, -most), most).astype(held_as)


def setup_inputs(seed: int = 0) -> dict:
    keys = jax.random.split(jax.random.key(seed), 7)
    tokens = normal_values(keys[0], (TOKENS, D), 1.0, 6.0, ((0, 16), (1, 2)))
    grad_out = normal_values(keys[1], (TOKENS, D), 1.0, 6.0, ((0, 16), (1, 2)))
    routing_keys = jax.random.split(jax.random.fold_in(keys[2], 1), TOKENS // TOK_GRP)
    routing_turns = jax.random.permutation(jax.random.fold_in(keys[2], 3), TOKENS // TOK_GRP)
    routing = jax.vmap(lambda own, number: routed_block(jax.random.fold_in(keys[2], 2), own, number, TOK_GRP, EXPERTS, TOPK, CAP, 2))(routing_keys, routing_turns).reshape((TOKENS, TOPK))
    gates = jnp.clip(0.1 + 0.9 * jax.random.uniform(keys[3], (TOKENS, TOPK), jnp.float32) ** block_scale(keys[3], (TOKENS, TOPK), ((0, 16),), -0.2, 0.2), 0.1, 1.0)
    w_in = normal_values(keys[4], (EXPERTS, D, 2, FF), D ** -0.5, 0.09375, ((0, 16), (3, 2)))
    w_out = normal_values(keys[5], (EXPERTS, FF, D), FF ** -0.5, 0.15625, ((0, 16), (1, 2)))
    return {"tokens": tokens, "grad_out": grad_out, "routing": routing, "gates": gates, "w_in": w_in, "w_out": w_out}


def reference(tokens, grad_out, routing, gates, w_in, w_out):
    groups = TOKENS // TOK_GRP
    slot_rows = groups * CAP
    hidden = FF // N_TENSOR
    grouped = routing.reshape(groups, TOK_GRP, TOPK)
    is_named = (grouped[..., None] == jnp.arange(EXPERTS, dtype=jnp.int32)).astype(jnp.int32)
    counts = jnp.sum(is_named, axis=2)
    before = jnp.cumsum(counts, axis=1) - counts
    slot_index = jnp.sum(is_named * before[:, :, None, :], axis=3).reshape(-1)
    expert_flat = routing.reshape(-1)
    group_flat = (jnp.arange(TOKENS * TOPK, dtype=jnp.int32) // (TOK_GRP * TOPK)).astype(jnp.int32)
    position = (group_flat * CAP + slot_index).astype(jnp.int32)
    table = jnp.full((EXPERTS, slot_rows), TOKENS * TOPK, jnp.int32)
    table = table.at[expert_flat, position].set(jnp.arange(TOKENS * TOPK, dtype=jnp.int32))
    x_rows = jnp.repeat(tokens, TOPK, axis=0)
    x_rows = jnp.concatenate([x_rows, jnp.zeros((1, D), tokens.dtype)], axis=0)
    scaled = (gates[:, :, None] * grad_out[:, None, :].astype(jnp.float32)).astype(jnp.bfloat16)
    scaled = jnp.concatenate([scaled.reshape(TOKENS * TOPK, D), jnp.zeros((1, D), jnp.bfloat16)], axis=0)

    def one_expert(expert_id):
        picks = table[expert_id]
        x_sel = x_rows[picks]
        dy_sel = scaled[picks]
        w_both = w_in[expert_id].reshape(D, 2 * FF)
        gate_up = jnp.dot(x_sel, w_both, preferred_element_type=jnp.float32)
        gate_proj = gate_up[:, :FF]
        up_proj = gate_up[:, FF:]
        sig_gate = jax.nn.sigmoid(gate_proj)
        activation = (gate_proj * sig_gate * up_proj).astype(jnp.bfloat16)
        act_grad = jnp.dot(dy_sel, w_out[expert_id].T, preferred_element_type=jnp.float32)
        grad_gate = act_grad * up_proj * sig_gate * (1.0 + gate_proj * (1.0 - sig_gate))
        grad_up = act_grad * gate_proj * sig_gate
        grad_both = jnp.concatenate([grad_gate, grad_up], axis=1).astype(jnp.bfloat16)
        act_slices = activation.astype(jnp.float32).reshape(slot_rows, N_TENSOR, hidden)
        down_slices = w_out[expert_id].astype(jnp.float32).reshape(N_TENSOR, hidden, D)
        out_parts = jnp.einsum('rsf,sfd->srd', act_slices, down_slices).astype(jnp.bfloat16)
        expert_out = jnp.sum(out_parts.astype(jnp.float32), axis=0)
        grad_slices = grad_both.astype(jnp.float32).reshape(slot_rows, 2, N_TENSOR, hidden)
        in_slices = w_in[expert_id].astype(jnp.float32).reshape(D, 2, N_TENSOR, hidden)
        in_parts = jnp.einsum('rcsf,dcsf->srd', grad_slices, in_slices).astype(jnp.bfloat16)
        input_grad = jnp.sum(in_parts.astype(jnp.float32), axis=0)
        grad_down = jnp.dot(activation.T, dy_sel, preferred_element_type=jnp.float32).astype(jnp.bfloat16)
        return expert_out, input_grad, grad_down

    expert_outs, input_grads, grad_w_out = lax.map(one_expert, jnp.arange(EXPERTS, dtype=jnp.int32))
    pair_out = expert_outs[expert_flat, position].reshape(TOKENS, TOPK, D)
    pair_in = input_grads[expert_flat, position].reshape(TOKENS, TOPK, D)
    mixed = jnp.sum(gates[:, :, None] * pair_out, axis=1).astype(jnp.bfloat16)
    grad_tokens = jnp.sum(pair_in, axis=1).astype(jnp.bfloat16)
    return mixed, grad_tokens, grad_w_out
```

```python
import functools

import jax
import jax.numpy as jnp
from jax import lax
from jax.experimental import pallas as pl
from jax.experimental.pallas import tpu as pltpu
from jax.sharding import PartitionSpec as P


def dispatched(tokens, grad_out, routing, gates, w_in, w_out):
    n_experts = lax.axis_size("expert")
    tok_rows = tokens.shape[0]
    topk_count = routing.shape[1]
    slot_cap = min(tok_rows, 16 * tok_rows // n_experts)
    slot_rows = n_experts * slot_cap
    model_width = w_out.shape[2]
    hidden = w_out.shape[1]
    experts = jnp.arange(n_experts, dtype=jnp.int32)
    is_named = (routing[:, :, None] == experts).astype(jnp.int32)
    counts = jnp.sum(is_named, axis=1)
    before = jnp.cumsum(counts, axis=0) - counts
    slot_index = jnp.sum(is_named * before[:, None, :], axis=2)
    target = (routing * slot_cap + slot_index).reshape(-1)
    placing = (jnp.arange(slot_rows, dtype=jnp.int32)[:, None] == target[None, :]).astype(
        jnp.bfloat16
    )
    scaled = (gates[:, :, None] * grad_out[:, None, :].astype(jnp.float32)).astype(jnp.bfloat16)
    scaled = scaled.reshape(tok_rows * topk_count, -1)
    sent_dy = jnp.dot(placing, scaled, preferred_element_type=jnp.float32).astype(jnp.bfloat16)
    w_both = w_in[0].reshape(model_width, 2 * hidden)
    w_down = w_out[0]
    contract_last = (((1,), (1,)), ((), ()))
    contract_first = (((0,), (0,)), ((), ()))
    whole = lax.all_gather(tokens, "tensor", axis=1, tiled=True)
    x_copies = jnp.repeat(whole, topk_count, axis=0)
    sent_x = jnp.dot(placing, x_copies, preferred_element_type=jnp.float32).astype(jnp.bfloat16)
    recv_x, recv_dy = (
        lax.all_to_all(sent_x, "expert", split_axis=0, concat_axis=0, tiled=True),
        lax.all_to_all(sent_dy, "expert", split_axis=0, concat_axis=0, tiled=True),
    )
    gate_up = jnp.dot(recv_x, w_both, preferred_element_type=jnp.float32)
    dy_piece = lax.all_gather(recv_dy, "tensor", axis=1, tiled=True)
    act_grad = lax.dot_general(dy_piece, w_down, contract_last, preferred_element_type=jnp.float32)
    dy_full = dy_piece
    act_grad, dy_full = (act_grad, dy_full)
    gate_proj = gate_up[:, :hidden]
    up_proj = gate_up[:, hidden:]
    sig_gate = jax.nn.sigmoid(gate_proj)
    activation = (gate_proj * sig_gate * up_proj).astype(jnp.bfloat16)
    grad_gate = act_grad * up_proj * sig_gate * (1.0 + gate_proj * (1.0 - sig_gate))
    grad_up = act_grad * gate_proj * sig_gate
    grad_both = jnp.concatenate([grad_gate, grad_up], axis=1).astype(jnp.bfloat16)
    out_part = jnp.dot(activation, w_down, preferred_element_type=jnp.float32)
    in_part = lax.dot_general(grad_both, w_both, contract_last, preferred_element_type=jnp.float32)
    grad_down = lax.dot_general(
        activation, dy_full, contract_first, preferred_element_type=jnp.float32
    )
    grad_down = grad_down.astype(jnp.bfloat16)[None]
    out_sum, in_sum = (
        lax.psum_scatter(
            out_part.astype(jnp.bfloat16), "tensor", scatter_dimension=1, tiled=True
        ).astype(jnp.float32),
        lax.psum_scatter(
            in_part.astype(jnp.bfloat16), "tensor", scatter_dimension=1, tiled=True
        ).astype(jnp.float32),
    )
    back_out, back_in = (
        lax.all_to_all(
            out_sum.astype(jnp.bfloat16), "expert", split_axis=0, concat_axis=0, tiled=True
        ).astype(out_sum.dtype),
        lax.all_to_all(
            in_sum.astype(jnp.bfloat16), "expert", split_axis=0, concat_axis=0, tiled=True
        ).astype(in_sum.dtype),
    )
    place_wide = placing.astype(jnp.float32)
    picked_out = lax.dot_general(
        place_wide,
        back_out,
        contract_first,
        precision=lax.Precision.HIGHEST,
        preferred_element_type=jnp.float32,
    )
    picked_in = lax.dot_general(
        place_wide,
        back_in,
        contract_first,
        precision=lax.Precision.HIGHEST,
        preferred_element_type=jnp.float32,
    )
    picked_out = picked_out.reshape(tok_rows, topk_count, -1)
    picked_in = picked_in.reshape(tok_rows, topk_count, -1)
    mixed = jnp.sum(gates[:, :, None] * picked_out, axis=1).astype(jnp.bfloat16)
    grad_tokens = jnp.sum(picked_in, axis=1).astype(jnp.bfloat16)
    return (mixed, grad_tokens, grad_down)

MESH = pl.DeviceIdType.MESH
F32 = jnp.float32
BF16 = jnp.bfloat16
NT = (((1,), (1,)), ((), ()))


def fused_kernel(
    n_z,
    tok_ref,
    dy_ref,
    gate_ref,
    w_in_hbm,
    w_out_hbm,
    mixed_ref,
    gtok_ref,
    gdown_hbm,
    buf,
    parts,
    sib_in,
    one_a,
    one_b,
    two,
    three,
    xs,
    scaled,
    gate_up,
    act_grad,
    act,
    act_t,
    grad_both,
    w_in,
    w_out,
    stage,
    w_sem,
    gz_send,
    gx_send,
    gy_send,
    gs_send,
    g_recv,
    s_send,
    s_recv,
    one_send,
    one_a_recv,
    one_b_recv,
    two_send,
    two_recv,
    three_send,
    three_recv,
    out_sem,
):
    rows, width = tok_ref.shape
    part = width // 2
    n_chips = 2 * n_z
    hidden = w_out.shape[0]
    expert = lax.axis_index("expert")
    y = lax.axis_index("tensor")
    core = lax.rem(expert, 2)
    x = lax.rem(expert // 2, 2)
    z = expert // 4
    other = 1 - core

    def expert_at(j, dx, c):
        return lax.rem(z + j, n_z) * 4 + lax.rem(x + dx, 2) * 2 + c

    def chip_at(j, dx):
        return lax.rem(z + j, n_z) * 2 + lax.rem(x + dx, 2)

    def quarter(dy, h):
        return lax.rem(y + dy, 2) * 2 + h

    to_x = (expert_at(0, 1, core), y)
    to_y = (expert, 1 - y)
    to_sib = (expert_at(0, 0, other), y)

    def to_z(j):
        return (expert_at(j, 0, core), y)

    load_in = pltpu.make_async_copy(w_in_hbm, w_in, w_sem.at[0])
    load_out = pltpu.make_async_copy(w_out_hbm, w_out, w_sem.at[1])
    load_in.start()
    load_out.start()

    barrier = pltpu.get_barrier_semaphore()
    partners = [to_z(j) for j in range(1, n_z)] + [to_x, to_y, to_sib]
    for partner in partners:
        pl.semaphore_signal(barrier, inc=1, device_id=partner, device_id_type=MESH)

    own = jnp.concatenate([tok_ref[...].astype(F32), dy_ref[...].astype(F32)], axis=0)
    for h in range(2):
        buf[expert, quarter(0, h)] = own[:, h * part : (h + 1) * part].astype(BF16)
    pl.semaphore_wait(barrier, len(partners))

    pending = []

    def send(src, dst, send_sem, recv_sem, target):
        copy = pltpu.make_async_remote_copy(
            src_ref=src,
            dst_ref=dst,
            send_sem=send_sem,
            recv_sem=recv_sem,
            device_id=target,
            device_id_type=MESH,
        )
        copy.start()
        pending.append(copy)
        return copy

    def pass_on(j, dx, dy, h, target, sem):
        e, q = expert_at(j, dx, core), quarter(dy, h)
        send(buf.at[e, q], buf.at[e, q], sem, g_recv.at[e, q], target)

    def arrived(j, dx, dy, h, c):
        e, q = expert_at(j, dx, c), quarter(dy, h)
        pltpu.make_async_remote_copy(
            src_ref=buf.at[e, q],
            dst_ref=buf.at[e, q],
            send_sem=gs_send.at[0],
            recv_sem=g_recv.at[e, q],
            device_id=to_sib,
            device_id_type=MESH,
        ).wait_recv()

    def to_sibling(j, dx, dy, h):
        pass_on(j, dx, dy, h, to_sib, gs_send.at[((j * 2 + dx) * 2 + dy) * 2 + h])

    def along_x(j, dy, h):
        pass_on(j, 0, dy, h, to_x, gx_send.at[(j * 2 + dy) * 2 + h])

    def along_y(j, dx, h):
        pass_on(j, dx, 0, h, to_y, gy_send.at[(j * 2 + dx) * 2 + h])

    def spread(j):
        for h in range(2):
            if j:
                arrived(j, 0, 0, h, core)
            along_x(j, 0, h)
            along_y(j, 0, h)
            to_sibling(j, 0, 0, h)

    def second(j):
        arrived(j, 1, 0, 0, core)
        along_y(j, 1, 0)
        to_sibling(j, 1, 0, 0)
        arrived(j, 0, 1, 1, core)
        along_x(j, 1, 1)
        to_sibling(j, 0, 1, 1)

    z_order = [1, n_z - 1] + list(range(2, n_z - 1))
    for h in range(2):
        for j in z_order:
            pass_on(0, 0, 0, h, to_z(j), gz_send.at[(j - 1) * 2 + h])
    spread(0)
    for j in z_order[:2]:
        spread(j)
    second(0)
    for j in z_order[2:]:
        spread(j)
    for j in z_order:
        second(j)

    def forward(dy, h, first):
        q = quarter(dy, h)

        def lay(p, carry):
            at = pl.ds(pl.multiple_of(p * (2 * rows), 2 * rows), 2 * rows)
            even = buf[2 * p, q].astype(F32)
            odd = buf[2 * p + 1, q].astype(F32)
            xs[at, :] = jnp.concatenate([even[:rows], odd[:rows]], axis=0).astype(BF16)
            both = jnp.concatenate([even[rows:], odd[rows:]], axis=0)
            scaled[q, at, :] = (gate_ref[at, 0:1] * both).astype(BF16)
            return carry

        lax.fori_loop(0, n_chips, lay, 0)
        if first:
            load_in.wait()
            load_out.wait()
        tile = 256
        deep = pl.ds(pl.multiple_of(q * part, part), part)

        def gates_up(n, carry):
            at = pl.ds(pl.multiple_of(n * tile, tile), tile)
            piece = jnp.dot(xs[...], w_in[deep, at], preferred_element_type=F32)
            gate_up[:, at] = piece if first else gate_up[:, at] + piece
            return carry

        lax.fori_loop(0, 2 * hidden // tile, gates_up, 0)

        def grads(n, carry):
            at = pl.ds(pl.multiple_of(n * tile, tile), tile)
            piece = lax.dot_general(scaled[q], w_out[at, deep], NT, preferred_element_type=F32)
            act_grad[:, at] = piece if first else act_grad[:, at] + piece
            return carry

        lax.fori_loop(0, hidden // tile, grads, 0)

    def from_sibling(dy, h):
        for j in range(n_z):
            for dx in range(2):
                arrived(j, dx, dy, h, other)

    def third(dy, h, dxs):
        for j in [0] + z_order:
            for dx in dxs:
                arrived(j, dx, dy, h, core)
                to_sibling(j, dx, dy, h)

    from_sibling(0, 0)
    forward(0, 0, True)
    third(0, 1, [1])
    from_sibling(0, 1)
    forward(0, 1, False)
    third(1, 0, [0, 1])
    third(1, 1, [1])
    from_sibling(1, 0)
    forward(1, 0, False)
    from_sibling(1, 1)
    forward(1, 1, False)

    def middle(r, carry):
        at = pl.ds(pl.multiple_of(r * (2 * rows), 2 * rows), 2 * rows)
        gate_proj = gate_up[at, :hidden]
        up_proj = gate_up[at, hidden:]
        grad = act_grad[at, :]
        sig = jax.nn.sigmoid(gate_proj)
        act[at, :] = (gate_proj * sig * up_proj).astype(BF16)
        grad_both[at, :hidden] = (grad * up_proj * sig * (1.0 + gate_proj * (1.0 - sig))).astype(BF16)
        grad_both[at, hidden:] = (grad * gate_proj * sig).astype(BF16)
        return carry

    lax.fori_loop(0, n_chips, middle, 0)

    def backward(dy, h):
        q = quarter(dy, h)
        tile = 256

        def step(n, carry):
            lanes = pl.ds(pl.multiple_of(n * tile, tile), tile)
            at = pl.ds(pl.multiple_of(q * part + n * tile, tile), tile)
            out = jnp.dot(act[...], w_out[:, at], preferred_element_type=F32) * gate_ref[:, 0:1]
            back = lax.dot_general(grad_both[...], w_in[at, :], NT, preferred_element_type=F32)
            for e in range(2 * n_chips):
                take = slice(e * rows, (e + 1) * rows)
                parts[e % 2, q, e // 2, :, lanes] = jnp.concatenate(
                    [out[take], back[take]], axis=0
                ).astype(BF16)
            return carry

        lax.fori_loop(0, part // tile, step, 0)
        return send(parts.at[other, q], sib_in.at[q], s_send.at[q], s_recv.at[q], to_sib)

    def chip_sum(dy, h, copy):
        q = quarter(dy, h)
        copy.wait_recv()

        def add(p, carry):
            parts[core, q, p] = (parts[core, q, p].astype(F32) + sib_in[q, p].astype(F32)).astype(BF16)
            return carry

        lax.fori_loop(0, n_chips, add, 0)

    def first_a(j, dx):
        p = chip_at(j, dx)
        return send(
            parts.at[core, quarter(1, 0), p],
            one_a.at[j * 2 + dx],
            one_send.at[j * 2 + dx],
            one_a_recv.at[j * 2 + dx],
            to_y,
        )

    def first_b(j, dy):
        k = j * 2 + dy
        return send(
            parts.at[core, quarter(dy, 1), chip_at(j, 1)],
            one_b.at[k],
            one_send.at[2 * n_z + k],
            one_b_recv.at[k],
            to_x,
        )

    far = [1 + k for k in range(n_z - 1)] + [0]
    a_copies, b_copies = {}, {}
    sib_a1 = backward(1, 0)
    sib_b1 = backward(1, 1)
    chip_sum(1, 0, sib_a1)
    for dx in (1, 0):
        for j in far:
            a_copies[j, dx] = first_a(j, dx)
    sib_b0 = backward(0, 1)
    chip_sum(1, 1, sib_b1)
    for j in far:
        b_copies[j, 1] = first_b(j, 1)
    sib_a0 = backward(0, 0)
    chip_sum(0, 1, sib_b0)
    for j in far:
        b_copies[j, 0] = first_b(j, 0)
    chip_sum(0, 0, sib_a0)

    act_t[...] = act[...].T

    out_copies = []

    def down_grad(q):
        tile = 256
        if q >= 2:
            out_copies[q - 2].wait()

        def step(n, carry):
            at = pl.ds(pl.multiple_of(n * tile, tile), tile)
            stage[q % 2, :, at] = jnp.dot(
                act_t[...], scaled[q, :, at], preferred_element_type=F32
            ).astype(BF16)
            return carry

        lax.fori_loop(0, part // tile, step, 0)
        copy = pltpu.make_async_copy(
            stage.at[q % 2], gdown_hbm.at[:, pl.ds(q * part, part)], out_sem.at[q]
        )
        copy.start()
        out_copies.append(copy)

    two_copies = {}
    for k, j in enumerate(far):
        if k < 4:
            down_grad(k)
        p = chip_at(j, 1)
        qa, qb = quarter(0, 0), quarter(1, 1)
        a_copies[j, 1].wait_recv()
        parts[core, qa, p] = (
            parts[core, qa, p].astype(F32) + one_a[j * 2 + 1].astype(F32)
        ).astype(BF16)
        two_copies[j, 0] = send(
            parts.at[core, qa, p], two.at[0, j], two_send.at[0, j], two_recv.at[0, j], to_x
        )
        p = chip_at(j, 0)
        b_copies[j, 1].wait_recv()
        parts[core, qb, p] = (
            parts[core, qb, p].astype(F32) + one_b[j * 2 + 1].astype(F32)
        ).astype(BF16)
        two_copies[j, 1] = send(
            parts.at[core, qb, p], two.at[1, j], two_send.at[1, j], two_recv.at[1, j], to_y
        )
    for k in range(len(out_copies), 4):
        down_grad(k)

    three_copies = {}
    for j in far:
        for h in range(2):
            q, p = quarter(0, h), chip_at(j, 0)
            first = (a_copies, b_copies)[h]
            held = (one_a, one_b)[h]
            first[j, 0].wait_recv()
            two_copies[j, h].wait_recv()
            total = (
                parts[core, q, p].astype(F32)
                + held[j * 2].astype(F32)
                + two[h, j].astype(F32)
            )
            if j:
                parts[core, q, p] = total.astype(BF16)
                three_copies[j, h] = send(
                    parts.at[core, q, p],
                    three.at[h, j - 1],
                    three_send.at[h, j - 1],
                    three_recv.at[h, j - 1],
                    to_z(j),
                )
            else:
                for i in range(1, n_z):
                    three_copies[i, h].wait_recv()
                    total = total + three[h, i - 1].astype(F32)
                lanes = slice(h * part, (h + 1) * part)
                mixed_ref[:, lanes] = total[:rows].astype(BF16)
                gtok_ref[:, lanes] = total[rows:].astype(BF16)

    for copy in pending:
        copy.wait_send()
    for copy in out_copies[-2:]:
        copy.wait()


def dense(tokens, grad_out, routing, gates, w_in, w_out):
    n_experts = lax.axis_size("expert")
    n_z = n_experts // 4
    rows, width = tokens.shape
    part = width // 2
    model_width, hidden = w_out.shape[2], w_out.shape[1]
    slots = n_experts * rows
    experts = jnp.arange(n_experts, dtype=jnp.int32)
    table = jnp.sum(
        jnp.where(routing[:, :, None] == experts, gates[:, :, None], 0.0), axis=1
    )
    table = lax.all_gather(table, "expert", axis=0, tiled=True)
    mine = jnp.sum(jnp.where(experts == lax.axis_index("expert"), table, 0.0), axis=1)
    gate = jnp.broadcast_to(mine[:, None], (slots, 128))
    w_both = w_in[0].reshape(model_width, 2 * hidden)
    vmem = pl.BlockSpec(memory_space=pltpu.VMEM)
    anywhere = pl.BlockSpec(memory_space=pl.ANY)
    block = (2 * rows, part)
    dma = pltpu.SemaphoreType.DMA
    flops = 2 * slots * model_width * hidden * 7
    mixed, gtok, gdown = pl.pallas_call(
        functools.partial(fused_kernel, n_z),
        out_shape=(
            jax.ShapeDtypeStruct((rows, width), BF16),
            jax.ShapeDtypeStruct((rows, width), BF16),
            jax.ShapeDtypeStruct((hidden, model_width), BF16),
        ),
        in_specs=[vmem, vmem, vmem, anywhere, anywhere],
        out_specs=(vmem, vmem, anywhere),
        scratch_shapes=[
            pltpu.VMEM((n_experts, 4) + block, BF16),
            pltpu.VMEM((2, 4, 2 * n_z) + block, BF16),
            pltpu.VMEM((4, 2 * n_z) + block, BF16),
            pltpu.VMEM((2 * n_z,) + block, BF16),
            pltpu.VMEM((2 * n_z,) + block, BF16),
            pltpu.VMEM((2, n_z) + block, BF16),
            pltpu.VMEM((2, n_z - 1) + block, BF16),
            pltpu.VMEM((slots, part), BF16),
            pltpu.VMEM((4, slots, part), BF16),
            pltpu.VMEM((slots, 2 * hidden), F32),
            pltpu.VMEM((slots, hidden), F32),
            pltpu.VMEM((slots, hidden), BF16),
            pltpu.VMEM((hidden, slots), BF16),
            pltpu.VMEM((slots, 2 * hidden), BF16),
            pltpu.VMEM((model_width, 2 * hidden), BF16),
            pltpu.VMEM((hidden, model_width), BF16),
            pltpu.VMEM((2, hidden, part), BF16),
            dma((2,)),
            dma((2 * (n_z - 1),)),
            dma((4 * n_z,)),
            dma((4 * n_z,)),
            dma((8 * n_z,)),
            dma((n_experts, 4)),
            dma((4,)),
            dma((4,)),
            dma((4 * n_z,)),
            dma((2 * n_z,)),
            dma((2 * n_z,)),
            dma((2, n_z)),
            dma((2, n_z)),
            dma((2, n_z - 1)),
            dma((2, n_z - 1)),
            dma((4,)),
        ],
        compiler_params=pltpu.CompilerParams(
            collective_id=0, has_side_effects=True, vmem_limit_bytes=60 * 1024 * 1024
        ),
        cost_estimate=pl.CostEstimate(
            flops=flops, bytes_accessed=8 * model_width * hidden, transcendentals=slots * hidden
        ),
    )(tokens, grad_out, gate, w_both, w_out[0])
    return mixed, gtok, gdown[None]


def shards(tokens, grad_out, routing, gates, w_in, w_out):
    n_experts = lax.axis_size("expert")
    rows = tokens.shape[0]
    whole_groups = 16 * rows // n_experts >= rows
    if whole_groups and n_experts % 4 == 0 and n_experts >= 16 and lax.axis_size("tensor") == 2:
        return dense(tokens, grad_out, routing, gates, w_in, w_out)
    return dispatched(tokens, grad_out, routing, gates, w_in, w_out)


def solution(mesh):
    in_specs = (
        P("expert", "tensor"),
        P("expert", "tensor"),
        P("expert", None),
        P("expert", None),
        P("expert", None, None, "tensor"),
        P("expert", "tensor", None),
    )
    out_specs = (P("expert", "tensor"), P("expert", "tensor"), P("expert", "tensor", None))
    return jax.shard_map(shards, mesh=mesh, in_specs=in_specs, out_specs=out_specs, check_vma=False)
```

```python
import functools

import jax
import jax.numpy as jnp
from jax import lax
from jax.experimental import pallas as pl
from jax.experimental.pallas import tpu as pltpu
from jax.sharding import PartitionSpec as P


def dispatched(tokens, grad_out, routing, gates, w_in, w_out):
    n_experts = lax.axis_size("expert")
    tok_rows = tokens.shape[0]
    topk_count = routing.shape[1]
    slot_cap = min(tok_rows, 16 * tok_rows // n_experts)
    slot_rows = n_experts * slot_cap
    model_width = w_out.shape[2]
    hidden = w_out.shape[1]
    experts = jnp.arange(n_experts, dtype=jnp.int32)
    is_named = (routing[:, :, None] == experts).astype(jnp.int32)
    counts = jnp.sum(is_named, axis=1)
    before = jnp.cumsum(counts, axis=0) - counts
    slot_index = jnp.sum(is_named * before[:, None, :], axis=2)
    target = (routing * slot_cap + slot_index).reshape(-1)
    placing = (jnp.arange(slot_rows, dtype=jnp.int32)[:, None] == target[None, :]).astype(
        jnp.bfloat16
    )
    scaled = (gates[:, :, None] * grad_out[:, None, :].astype(jnp.float32)).astype(jnp.bfloat16)
    scaled = scaled.reshape(tok_rows * topk_count, -1)
    sent_dy = jnp.dot(placing, scaled, preferred_element_type=jnp.float32).astype(jnp.bfloat16)
    w_both = w_in[0].reshape(model_width, 2 * hidden)
    w_down = w_out[0]
    contract_last = (((1,), (1,)), ((), ()))
    contract_first = (((0,), (0,)), ((), ()))
    whole = lax.all_gather(tokens, "tensor", axis=1, tiled=True)
    x_copies = jnp.repeat(whole, topk_count, axis=0)
    sent_x = jnp.dot(placing, x_copies, preferred_element_type=jnp.float32).astype(jnp.bfloat16)
    recv_x, recv_dy = (
        lax.all_to_all(sent_x, "expert", split_axis=0, concat_axis=0, tiled=True),
        lax.all_to_all(sent_dy, "expert", split_axis=0, concat_axis=0, tiled=True),
    )
    gate_up = jnp.dot(recv_x, w_both, preferred_element_type=jnp.float32)
    dy_piece = lax.all_gather(recv_dy, "tensor", axis=1, tiled=True)
    act_grad = lax.dot_general(dy_piece, w_down, contract_last, preferred_element_type=jnp.float32)
    dy_full = dy_piece
    act_grad, dy_full = (act_grad, dy_full)
    gate_proj = gate_up[:, :hidden]
    up_proj = gate_up[:, hidden:]
    sig_gate = jax.nn.sigmoid(gate_proj)
    activation = (gate_proj * sig_gate * up_proj).astype(jnp.bfloat16)
    grad_gate = act_grad * up_proj * sig_gate * (1.0 + gate_proj * (1.0 - sig_gate))
    grad_up = act_grad * gate_proj * sig_gate
    grad_both = jnp.concatenate([grad_gate, grad_up], axis=1).astype(jnp.bfloat16)
    out_part = jnp.dot(activation, w_down, preferred_element_type=jnp.float32)
    in_part = lax.dot_general(grad_both, w_both, contract_last, preferred_element_type=jnp.float32)
    grad_down = lax.dot_general(
        activation, dy_full, contract_first, preferred_element_type=jnp.float32
    )
    grad_down = grad_down.astype(jnp.bfloat16)[None]
    out_sum, in_sum = (
        lax.psum_scatter(
            out_part.astype(jnp.bfloat16), "tensor", scatter_dimension=1, tiled=True
        ).astype(jnp.float32),
        lax.psum_scatter(
            in_part.astype(jnp.bfloat16), "tensor", scatter_dimension=1, tiled=True
        ).astype(jnp.float32),
    )
    back_out, back_in = (
        lax.all_to_all(
            out_sum.astype(jnp.bfloat16), "expert", split_axis=0, concat_axis=0, tiled=True
        ).astype(out_sum.dtype),
        lax.all_to_all(
            in_sum.astype(jnp.bfloat16), "expert", split_axis=0, concat_axis=0, tiled=True
        ).astype(in_sum.dtype),
    )
    place_wide = placing.astype(jnp.float32)
    picked_out = lax.dot_general(
        place_wide,
        back_out,
        contract_first,
        precision=lax.Precision.HIGHEST,
        preferred_element_type=jnp.float32,
    )
    picked_in = lax.dot_general(
        place_wide,
        back_in,
        contract_first,
        precision=lax.Precision.HIGHEST,
        preferred_element_type=jnp.float32,
    )
    picked_out = picked_out.reshape(tok_rows, topk_count, -1)
    picked_in = picked_in.reshape(tok_rows, topk_count, -1)
    mixed = jnp.sum(gates[:, :, None] * picked_out, axis=1).astype(jnp.bfloat16)
    grad_tokens = jnp.sum(picked_in, axis=1).astype(jnp.bfloat16)
    return (mixed, grad_tokens, grad_down)

MESH = pl.DeviceIdType.MESH
F32 = jnp.float32
BF16 = jnp.bfloat16
NT = (((1,), (1,)), ((), ()))


def fused_kernel(
    n_z,
    tok_ref,
    dy_ref,
    routing_ref,
    gates_ref,
    w_in_hbm,
    w_out_hbm,
    mixed_ref,
    gtok_ref,
    act_t_hbm,
    scaled_hbm,
    tables,
    gate_ref,
    raw,
    buf,
    parts,
    sib_in,
    one_a,
    one_b,
    two,
    three,
    xs,
    scaled,
    gate_up,
    act_grad,
    act,
    act_t,
    grad_both,
    w_in,
    w_out,
    w_sem,
    raw_sem,
    tz_send,
    tx_send,
    ts_send,
    t_recv,
    gz_send,
    gx_send,
    gy_send,
    gs_send,
    g_recv,
    s_send,
    s_recv,
    one_send,
    one_a_recv,
    one_b_recv,
    two_send,
    two_recv,
    three_send,
    three_recv,
    out_sem,
):
    rows, width = tok_ref.shape
    part = width // 2
    n_chips = 2 * n_z
    hidden = w_out.shape[0]
    expert = lax.axis_index("expert")
    y = lax.axis_index("tensor")
    core = lax.rem(expert, 2)
    x = lax.rem(expert // 2, 2)
    z = expert // 4
    other = 1 - core

    def expert_at(j, dx, c):
        return lax.rem(z + j, n_z) * 4 + lax.rem(x + dx, 2) * 2 + c

    def chip_at(j, dx):
        return lax.rem(z + j, n_z) * 2 + lax.rem(x + dx, 2)

    def quarter(dy, h):
        return lax.rem(y + dy, 2) * 2 + h

    to_x = (expert_at(0, 1, core), y)
    to_y = (expert, 1 - y)
    to_sib = (expert_at(0, 0, other), y)

    def to_z(j):
        return (expert_at(j, 0, core), y)

    depth = raw.shape[1]
    n_loads = w_in_hbm.shape[0] // depth

    def load(i):
        return pltpu.make_async_copy(
            w_in_hbm.at[pl.ds(i * depth, depth)], raw.at[i % 2], raw_sem.at[i % 2]
        )

    load_out = pltpu.make_async_copy(w_out_hbm, w_out, w_sem.at[0])
    load(0).start()
    load(1).start()
    load_out.start()

    def split(i):
        load(i).wait()
        some = 64

        def step(k, carry):
            at = pl.ds(pl.multiple_of(k * some, some), some)
            to = pl.ds(pl.multiple_of(i * depth + k * some, some), some)
            w_in[to, :] = raw[i % 2, at].reshape(some, 2 * hidden)
            return carry

        lax.fori_loop(0, depth // some, step, 0)
        if i + 2 < n_loads:
            load(i + 2).start()

    barrier = pltpu.get_barrier_semaphore()
    partners = [to_z(j) for j in range(1, n_z)] + [to_x, to_y, to_sib]
    for partner in partners:
        pl.semaphore_signal(barrier, inc=1, device_id=partner, device_id_type=MESH)

    own = jnp.concatenate([tok_ref[...].astype(F32), dy_ref[...].astype(F32)], axis=0)
    for h in range(2):
        buf[expert, quarter(0, h)] = own[:, h * part : (h + 1) * part].astype(BF16)
    lanes_of = lax.broadcasted_iota(jnp.int32, (rows, 128), 1)
    named, weight = routing_ref[...], gates_ref[...]
    table = jnp.zeros((rows, 128), F32)
    for k in range(named.shape[1]):
        table += jnp.where(named[:, k : k + 1] == lanes_of, weight[:, k : k + 1], 0.0)
    tables[expert] = table
    pl.semaphore_wait(barrier, len(partners))

    pending = []

    def send(src, dst, send_sem, recv_sem, target):
        copy = pltpu.make_async_remote_copy(
            src_ref=src,
            dst_ref=dst,
            send_sem=send_sem,
            recv_sem=recv_sem,
            device_id=target,
            device_id_type=MESH,
        )
        copy.start()
        pending.append(copy)
        return copy

    def pass_on(j, dx, dy, h, target, sem):
        e, q = expert_at(j, dx, core), quarter(dy, h)
        send(buf.at[e, q], buf.at[e, q], sem, g_recv.at[e, q], target)

    def arrived(j, dx, dy, h, c):
        e, q = expert_at(j, dx, c), quarter(dy, h)
        pltpu.make_async_remote_copy(
            src_ref=buf.at[e, q],
            dst_ref=buf.at[e, q],
            send_sem=gs_send.at[0],
            recv_sem=g_recv.at[e, q],
            device_id=to_sib,
            device_id_type=MESH,
        ).wait_recv()

    def to_sibling(j, dx, dy, h):
        pass_on(j, dx, dy, h, to_sib, gs_send.at[((j * 2 + dx) * 2 + dy) * 2 + h])

    def along_x(j, dy, h):
        pass_on(j, 0, dy, h, to_x, gx_send.at[(j * 2 + dy) * 2 + h])

    def along_y(j, dx, h):
        pass_on(j, dx, 0, h, to_y, gy_send.at[(j * 2 + dx) * 2 + h])

    def pass_table(j, dx, target, sem):
        e = expert_at(j, dx, core)
        send(tables.at[e], tables.at[e], sem, t_recv.at[e], target)

    def table_arrived(j, dx, c):
        e = expert_at(j, dx, c)
        pltpu.make_async_remote_copy(
            src_ref=tables.at[e],
            dst_ref=tables.at[e],
            send_sem=ts_send.at[0],
            recv_sem=t_recv.at[e],
            device_id=to_sib,
            device_id_type=MESH,
        ).wait_recv()

    def spread(j, h):
        if j:
            arrived(j, 0, 0, h, core)
        along_x(j, 0, h)
        along_y(j, 0, h)
        to_sibling(j, 0, 0, h)

    def spread_table(j):
        if j:
            table_arrived(j, 0, core)
        pass_table(j, 0, to_x, tx_send.at[j])
        pass_table(j, 0, to_sib, ts_send.at[2 * j])

    def second_a(j):
        arrived(j, 1, 0, 0, core)
        along_y(j, 1, 0)
        to_sibling(j, 1, 0, 0)

    def second_b(j):
        arrived(j, 0, 1, 1, core)
        along_x(j, 1, 1)
        to_sibling(j, 0, 1, 1)

    z_order = [1, n_z - 1] + list(range(2, n_z - 1))
    near, rest = z_order[:2], z_order[2:]
    for j in z_order:
        pass_table(0, 0, to_z(j), tz_send.at[j - 1])
    for h in range(2):
        for j in z_order:
            pass_on(0, 0, 0, h, to_z(j), gz_send.at[(j - 1) * 2 + h])
    spread(0, 0)
    spread(0, 1)
    spread_table(0)
    per = -(-n_loads // 4)

    def split_some(k):
        for i in range(k * per, min((k + 1) * per, n_loads)):
            split(i)

    split_some(0)
    for j in near:
        spread_table(j)
        spread(j, 0)
    second_a(0)
    second_b(0)
    split_some(1)
    for j in rest:
        spread_table(j)
        spread(j, 0)
    for j in near:
        second_a(j)
    split_some(2)
    for j in near:
        spread(j, 1)
    for j in rest:
        second_a(j)
    split_some(3)
    for j in rest:
        spread(j, 1)
    for j in z_order:
        second_b(j)
    for j in range(n_z):
        table_arrived(j, 1, core)
        pass_table(j, 1, to_sib, ts_send.at[2 * j + 1])
    for j in range(n_z):
        for dx in range(2):
            table_arrived(j, dx, other)
    for e in range(2 * n_chips):
        mine = jnp.sum(jnp.where(lanes_of == expert, tables[e], 0.0), axis=1, keepdims=True)
        gate_ref[e * rows : (e + 1) * rows, :] = jnp.broadcast_to(mine, (rows, 128))

    keep_scaled = []

    def forward(dy, h, first):
        q = quarter(dy, h)

        def lay(p, carry):
            at = pl.ds(pl.multiple_of(p * (2 * rows), 2 * rows), 2 * rows)
            even = buf[2 * p, q].astype(F32)
            odd = buf[2 * p + 1, q].astype(F32)
            xs[at, :] = jnp.concatenate([even[:rows], odd[:rows]], axis=0).astype(BF16)
            both = jnp.concatenate([even[rows:], odd[rows:]], axis=0)
            scaled[q, at, :] = (gate_ref[at, 0:1] * both).astype(BF16)
            return carry

        lax.fori_loop(0, n_chips, lay, 0)
        k = len(keep_scaled)
        copy = pltpu.make_async_copy(scaled.at[q], scaled_hbm.at[q], out_sem.at[k])
        copy.start()
        keep_scaled.append(copy)
        if first:
            load_out.wait()
        tile = 256
        deep = pl.ds(pl.multiple_of(q * part, part), part)

        def gates_up(n, carry):
            at = pl.ds(pl.multiple_of(n * tile, tile), tile)
            piece = jnp.dot(xs[...], w_in[deep, at], preferred_element_type=F32)
            gate_up[:, at] = piece if first else gate_up[:, at] + piece
            return carry

        lax.fori_loop(0, 2 * hidden // tile, gates_up, 0)

        def grads(n, carry):
            at = pl.ds(pl.multiple_of(n * tile, tile), tile)
            piece = lax.dot_general(scaled[q], w_out[at, deep], NT, preferred_element_type=F32)
            act_grad[:, at] = piece if first else act_grad[:, at] + piece
            return carry

        lax.fori_loop(0, hidden // tile, grads, 0)

    def from_sibling(dy, h):
        for j in range(n_z):
            for dx in range(2):
                arrived(j, dx, dy, h, other)

    def third(dy, h, dxs):
        for j in [0] + z_order:
            for dx in dxs:
                arrived(j, dx, dy, h, core)
                to_sibling(j, dx, dy, h)

    from_sibling(0, 0)
    forward(0, 0, True)
    third(0, 1, [1])
    from_sibling(0, 1)
    forward(0, 1, False)
    third(1, 0, [0, 1])
    third(1, 1, [1])
    from_sibling(1, 0)
    forward(1, 0, False)
    from_sibling(1, 1)
    forward(1, 1, False)

    def middle(r, carry):
        at = pl.ds(pl.multiple_of(r * (2 * rows), 2 * rows), 2 * rows)
        gate_proj = gate_up[at, :hidden]
        up_proj = gate_up[at, hidden:]
        grad = act_grad[at, :]
        sig = jax.nn.sigmoid(gate_proj)
        act[at, :] = (gate_proj * sig * up_proj).astype(BF16)
        grad_both[at, :hidden] = (grad * up_proj * sig * (1.0 + gate_proj * (1.0 - sig))).astype(BF16)
        grad_both[at, hidden:] = (grad * gate_proj * sig).astype(BF16)
        return carry

    lax.fori_loop(0, n_chips, middle, 0)

    def backward(dy, h, part_at):
        q = quarter(dy, h)
        tile = 256
        steps = part // tile // 2

        def step(n, carry):
            lanes = pl.ds(pl.multiple_of(n * tile, tile), tile)
            at = pl.ds(pl.multiple_of(q * part + n * tile, tile), tile)
            out = jnp.dot(act[...], w_out[:, at], preferred_element_type=F32) * gate_ref[:, 0:1]
            back = lax.dot_general(grad_both[...], w_in[at, :], NT, preferred_element_type=F32)
            for e in range(2 * n_chips):
                take = slice(e * rows, (e + 1) * rows)
                parts[e % 2, q, e // 2, :, lanes] = jnp.concatenate(
                    [out[take], back[take]], axis=0
                ).astype(BF16)
            return carry

        lax.fori_loop(part_at * steps, (part_at + 1) * steps, step, 0)
        lanes = pl.ds(part_at * (part // 2), part // 2)
        sib_copies[dy, h, part_at] = send(
            parts.at[other, q, :, :, lanes],
            sib_in.at[q, :, :, lanes],
            s_send.at[q, part_at],
            s_recv.at[q, part_at],
            to_sib,
        )

    def chip_sum(dy, h):
        q = quarter(dy, h)
        sib_copies[dy, h, 0].wait_recv()
        sib_copies[dy, h, 1].wait_recv()

        def add(p, carry):
            parts[core, q, p] = (parts[core, q, p].astype(F32) + sib_in[q, p].astype(F32)).astype(BF16)
            return carry

        lax.fori_loop(0, n_chips, add, 0)

    def first_a(j, dx):
        p = chip_at(j, dx)
        return send(
            parts.at[core, quarter(1, 0), p],
            one_a.at[j * 2 + dx],
            one_send.at[j * 2 + dx],
            one_a_recv.at[j * 2 + dx],
            to_y,
        )

    def first_b(j, dy):
        k = j * 2 + dy
        return send(
            parts.at[core, quarter(dy, 1), chip_at(j, 1)],
            one_b.at[k],
            one_send.at[2 * n_z + k],
            one_b_recv.at[k],
            to_x,
        )

    far = [1 + k for k in range(n_z - 1)] + [0]
    a_copies, b_copies, sib_copies = {}, {}, {}
    backward(1, 0, 0)
    backward(1, 0, 1)
    backward(1, 1, 0)
    chip_sum(1, 0)
    for dx in (1, 0):
        for j in far:
            a_copies[j, dx] = first_a(j, dx)
    backward(1, 1, 1)
    backward(0, 1, 0)
    chip_sum(1, 1)
    for j in far:
        b_copies[j, 1] = first_b(j, 1)
    backward(0, 1, 1)
    backward(0, 0, 0)
    chip_sum(0, 1)
    for j in far:
        b_copies[j, 0] = first_b(j, 0)
    backward(0, 0, 1)
    chip_sum(0, 0)

    keep_act = pltpu.make_async_copy(act_t, act_t_hbm, w_sem.at[1])
    two_copies = {}
    for k, j in enumerate(far):
        if k == len(far) - 1:
            act_t[...] = act[...].T
            keep_act.start()
        p = chip_at(j, 1)
        qa, qb = quarter(0, 0), quarter(1, 1)
        a_copies[j, 1].wait_recv()
        parts[core, qa, p] = (
            parts[core, qa, p].astype(F32) + one_a[j * 2 + 1].astype(F32)
        ).astype(BF16)
        two_copies[j, 0] = send(
            parts.at[core, qa, p], two.at[0, j], two_send.at[0, j], two_recv.at[0, j], to_x
        )
        p = chip_at(j, 0)
        b_copies[j, 1].wait_recv()
        parts[core, qb, p] = (
            parts[core, qb, p].astype(F32) + one_b[j * 2 + 1].astype(F32)
        ).astype(BF16)
        two_copies[j, 1] = send(
            parts.at[core, qb, p], two.at[1, j], two_send.at[1, j], two_recv.at[1, j], to_y
        )

    three_copies = {}
    for j in far:
        for h in range(2):
            q, p = quarter(0, h), chip_at(j, 0)
            first = (a_copies, b_copies)[h]
            held = (one_a, one_b)[h]
            first[j, 0].wait_recv()
            two_copies[j, h].wait_recv()
            total = (
                parts[core, q, p].astype(F32)
                + held[j * 2].astype(F32)
                + two[h, j].astype(F32)
            )
            if j:
                parts[core, q, p] = total.astype(BF16)
                three_copies[j, h] = send(
                    parts.at[core, q, p],
                    three.at[h, j - 1],
                    three_send.at[h, j - 1],
                    three_recv.at[h, j - 1],
                    to_z(j),
                )
            else:
                for i in range(1, n_z):
                    three_copies[i, h].wait_recv()
                    total = total + three[h, i - 1].astype(F32)
                lanes = slice(h * part, (h + 1) * part)
                mixed_ref[:, lanes] = total[:rows].astype(BF16)
                gtok_ref[:, lanes] = total[rows:].astype(BF16)

    for copy in pending:
        copy.wait_send()
    for copy in keep_scaled:
        copy.wait()
    keep_act.wait()


def last_kernel(act_t_ref, scaled_ref, mixed_in, gtok_in, mixed_ref, gtok_ref, gdown_ref):
    @pl.when(pl.program_id(0) == 0)
    def _():
        mixed_ref[...] = mixed_in[...]
        gtok_ref[...] = gtok_in[...]

    gdown_ref[...] = jnp.dot(act_t_ref[...], scaled_ref[0], preferred_element_type=F32).astype(BF16)


def dense(tokens, grad_out, routing, gates, w_in, w_out):
    n_experts = lax.axis_size("expert")
    n_z = n_experts // 4
    rows, width = tokens.shape
    part = width // 2
    model_width, hidden = w_out.shape[2], w_out.shape[1]
    slots = n_experts * rows
    vmem = pl.BlockSpec(memory_space=pltpu.VMEM)
    anywhere = pl.BlockSpec(memory_space=pl.ANY)
    block = (2 * rows, part)
    dma = pltpu.SemaphoreType.DMA
    flops = 2 * slots * model_width * hidden * 7
    depth = max(model_width // 8, 64)
    mixed, gtok, act_t, scaled = pl.pallas_call(
        functools.partial(fused_kernel, n_z),
        out_shape=(
            jax.ShapeDtypeStruct((rows, width), BF16),
            jax.ShapeDtypeStruct((rows, width), BF16),
            jax.ShapeDtypeStruct((hidden, slots), BF16),
            jax.ShapeDtypeStruct((4, slots, part), BF16),
        ),
        in_specs=[vmem, vmem, vmem, vmem, anywhere, anywhere],
        out_specs=(vmem, vmem, anywhere, anywhere),
        scratch_shapes=[
            pltpu.VMEM((n_experts, rows, 128), F32),
            pltpu.VMEM((slots, 128), F32),
            pltpu.VMEM((2, depth, 2, hidden), BF16),
            pltpu.VMEM((n_experts, 4) + block, BF16),
            pltpu.VMEM((2, 4, 2 * n_z) + block, BF16),
            pltpu.VMEM((4, 2 * n_z) + block, BF16),
            pltpu.VMEM((2 * n_z,) + block, BF16),
            pltpu.VMEM((2 * n_z,) + block, BF16),
            pltpu.VMEM((2, n_z) + block, BF16),
            pltpu.VMEM((2, n_z - 1) + block, BF16),
            pltpu.VMEM((slots, part), BF16),
            pltpu.VMEM((4, slots, part), BF16),
            pltpu.VMEM((slots, 2 * hidden), F32),
            pltpu.VMEM((slots, hidden), F32),
            pltpu.VMEM((slots, hidden), BF16),
            pltpu.VMEM((hidden, slots), BF16),
            pltpu.VMEM((slots, 2 * hidden), BF16),
            pltpu.VMEM((model_width, 2 * hidden), BF16),
            pltpu.VMEM((hidden, model_width), BF16),
            dma((2,)),
            dma((2,)),
            dma((n_z - 1,)),
            dma((n_z,)),
            dma((2 * n_z,)),
            dma((n_experts,)),
            dma((2 * (n_z - 1),)),
            dma((4 * n_z,)),
            dma((4 * n_z,)),
            dma((8 * n_z,)),
            dma((n_experts, 4)),
            dma((4, 2)),
            dma((4, 2)),
            dma((4 * n_z,)),
            dma((2 * n_z,)),
            dma((2 * n_z,)),
            dma((2, n_z)),
            dma((2, n_z)),
            dma((2, n_z - 1)),
            dma((2, n_z - 1)),
            dma((4,)),
        ],
        compiler_params=pltpu.CompilerParams(
            collective_id=0, has_side_effects=True, vmem_limit_bytes=60 * 1024 * 1024
        ),
        cost_estimate=pl.CostEstimate(
            flops=flops, bytes_accessed=8 * model_width * hidden, transcendentals=slots * hidden
        ),
    )(tokens, grad_out, routing, gates, w_in[0], w_out[0])
    tile = part // 2
    whole = pl.BlockSpec((rows, width), lambda n: (0, 0))
    mixed, gtok, gdown = pl.pallas_call(
        last_kernel,
        grid=(8,),
        out_shape=(
            jax.ShapeDtypeStruct((rows, width), BF16),
            jax.ShapeDtypeStruct((rows, width), BF16),
            jax.ShapeDtypeStruct((hidden, model_width), BF16),
        ),
        in_specs=[
            pl.BlockSpec((hidden, slots), lambda n: (0, 0)),
            pl.BlockSpec((1, slots, tile), lambda n: (n // 2, 0, n % 2)),
            whole,
            whole,
        ],
        out_specs=(whole, whole, pl.BlockSpec((hidden, tile), lambda n: (0, n))),
        compiler_params=pltpu.CompilerParams(vmem_limit_bytes=32 * 1024 * 1024),
        cost_estimate=pl.CostEstimate(
            flops=flops // 7, bytes_accessed=4 * model_width * hidden, transcendentals=0
        ),
    )(act_t, scaled, mixed, gtok)
    return mixed, gtok, gdown[None]


def shards(tokens, grad_out, routing, gates, w_in, w_out):
    n_experts = lax.axis_size("expert")
    rows = tokens.shape[0]
    whole_groups = 16 * rows // n_experts >= rows
    if whole_groups and n_experts % 4 == 0 and n_experts >= 16 and lax.axis_size("tensor") == 2:
        return dense(tokens, grad_out, routing, gates, w_in, w_out)
    return dispatched(tokens, grad_out, routing, gates, w_in, w_out)


def solution(mesh):
    in_specs = (
        P("expert", "tensor"),
        P("expert", "tensor"),
        P("expert", None),
        P("expert", None),
        P("expert", None, None, "tensor"),
        P("expert", "tensor", None),
    )
    out_specs = (P("expert", "tensor"), P("expert", "tensor"), P("expert", "tensor", None))
    return jax.shard_map(shards, mesh=mesh, in_specs=in_specs, out_specs=out_specs, check_vma=False)
```

```python
import functools

import jax
import jax.numpy as jnp
from jax import lax
from jax.experimental import pallas as pl
from jax.experimental.pallas import tpu as pltpu
from jax.sharding import PartitionSpec as P


def dispatched(tokens, grad_out, routing, gates, w_in, w_out):
    n_experts = lax.axis_size("expert")
    tok_rows = tokens.shape[0]
    topk_count = routing.shape[1]
    slot_cap = min(tok_rows, 16 * tok_rows // n_experts)
    slot_rows = n_experts * slot_cap
    model_width = w_out.shape[2]
    hidden = w_out.shape[1]
    experts = jnp.arange(n_experts, dtype=jnp.int32)
    is_named = (routing[:, :, None] == experts).astype(jnp.int32)
    counts = jnp.sum(is_named, axis=1)
    before = jnp.cumsum(counts, axis=0) - counts
    slot_index = jnp.sum(is_named * before[:, None, :], axis=2)
    target = (routing * slot_cap + slot_index).reshape(-1)
    placing = (jnp.arange(slot_rows, dtype=jnp.int32)[:, None] == target[None, :]).astype(
        jnp.bfloat16
    )
    scaled = (gates[:, :, None] * grad_out[:, None, :].astype(jnp.float32)).astype(jnp.bfloat16)
    scaled = scaled.reshape(tok_rows * topk_count, -1)
    sent_dy = jnp.dot(placing, scaled, preferred_element_type=jnp.float32).astype(jnp.bfloat16)
    w_both = w_in[0].reshape(model_width, 2 * hidden)
    w_down = w_out[0]
    contract_last = (((1,), (1,)), ((), ()))
    contract_first = (((0,), (0,)), ((), ()))
    whole = lax.all_gather(tokens, "tensor", axis=1, tiled=True)
    x_copies = jnp.repeat(whole, topk_count, axis=0)
    sent_x = jnp.dot(placing, x_copies, preferred_element_type=jnp.float32).astype(jnp.bfloat16)
    recv_x, recv_dy = (
        lax.all_to_all(sent_x, "expert", split_axis=0, concat_axis=0, tiled=True),
        lax.all_to_all(sent_dy, "expert", split_axis=0, concat_axis=0, tiled=True),
    )
    gate_up = jnp.dot(recv_x, w_both, preferred_element_type=jnp.float32)
    dy_piece = lax.all_gather(recv_dy, "tensor", axis=1, tiled=True)
    act_grad = lax.dot_general(dy_piece, w_down, contract_last, preferred_element_type=jnp.float32)
    dy_full = dy_piece
    act_grad, dy_full = (act_grad, dy_full)
    gate_proj = gate_up[:, :hidden]
    up_proj = gate_up[:, hidden:]
    sig_gate = jax.nn.sigmoid(gate_proj)
    activation = (gate_proj * sig_gate * up_proj).astype(jnp.bfloat16)
    grad_gate = act_grad * up_proj * sig_gate * (1.0 + gate_proj * (1.0 - sig_gate))
    grad_up = act_grad * gate_proj * sig_gate
    grad_both = jnp.concatenate([grad_gate, grad_up], axis=1).astype(jnp.bfloat16)
    out_part = jnp.dot(activation, w_down, preferred_element_type=jnp.float32)
    in_part = lax.dot_general(grad_both, w_both, contract_last, preferred_element_type=jnp.float32)
    grad_down = lax.dot_general(
        activation, dy_full, contract_first, preferred_element_type=jnp.float32
    )
    grad_down = grad_down.astype(jnp.bfloat16)[None]
    out_sum, in_sum = (
        lax.psum_scatter(
            out_part.astype(jnp.bfloat16), "tensor", scatter_dimension=1, tiled=True
        ).astype(jnp.float32),
        lax.psum_scatter(
            in_part.astype(jnp.bfloat16), "tensor", scatter_dimension=1, tiled=True
        ).astype(jnp.float32),
    )
    back_out, back_in = (
        lax.all_to_all(
            out_sum.astype(jnp.bfloat16), "expert", split_axis=0, concat_axis=0, tiled=True
        ).astype(out_sum.dtype),
        lax.all_to_all(
            in_sum.astype(jnp.bfloat16), "expert", split_axis=0, concat_axis=0, tiled=True
        ).astype(in_sum.dtype),
    )
    place_wide = placing.astype(jnp.float32)
    picked_out = lax.dot_general(
        place_wide,
        back_out,
        contract_first,
        precision=lax.Precision.HIGHEST,
        preferred_element_type=jnp.float32,
    )
    picked_in = lax.dot_general(
        place_wide,
        back_in,
        contract_first,
        precision=lax.Precision.HIGHEST,
        preferred_element_type=jnp.float32,
    )
    picked_out = picked_out.reshape(tok_rows, topk_count, -1)
    picked_in = picked_in.reshape(tok_rows, topk_count, -1)
    mixed = jnp.sum(gates[:, :, None] * picked_out, axis=1).astype(jnp.bfloat16)
    grad_tokens = jnp.sum(picked_in, axis=1).astype(jnp.bfloat16)
    return (mixed, grad_tokens, grad_down)

MESH = pl.DeviceIdType.MESH
F32 = jnp.float32
BF16 = jnp.bfloat16
NT = (((1,), (1,)), ((), ()))


def fused_kernel(
    n_z,
    tok_ref,
    dy_ref,
    routing_ref,
    gates_ref,
    w_in_hbm,
    w_out_hbm,
    mixed_ref,
    gtok_ref,
    act_t_hbm,
    scaled_hbm,
    tables,
    gate_ref,
    raw,
    buf,
    parts,
    sib_in,
    one_a,
    one_b,
    two,
    three,
    xs,
    scaled,
    gate_up,
    act_grad,
    act,
    act_t,
    grad_both,
    w_in,
    w_out,
    w_sem,
    raw_sem,
    tz_send,
    tx_send,
    ts_send,
    t_recv,
    gz_send,
    gx_send,
    gy_send,
    gs_send,
    g_recv,
    s_send,
    s_recv,
    one_send,
    one_a_recv,
    one_b_recv,
    two_send,
    two_recv,
    three_send,
    three_recv,
    out_sem,
):
    rows, width = tok_ref.shape
    part = width // 2
    n_chips = 2 * n_z
    hidden = w_out.shape[0]
    expert = lax.axis_index("expert")
    y = lax.axis_index("tensor")
    core = lax.rem(expert, 2)
    x = lax.rem(expert // 2, 2)
    z = expert // 4
    other = 1 - core

    def expert_at(j, dx, c):
        return lax.rem(z + j, n_z) * 4 + lax.rem(x + dx, 2) * 2 + c

    def chip_at(j, dx):
        return lax.rem(z + j, n_z) * 2 + lax.rem(x + dx, 2)

    def quarter(dy, h):
        return lax.rem(y + dy, 2) * 2 + h

    to_x = (expert_at(0, 1, core), y)
    to_y = (expert, 1 - y)
    to_sib = (expert_at(0, 0, other), y)

    def to_z(j):
        return (expert_at(j, 0, core), y)

    depth = raw.shape[1]
    n_loads = w_in_hbm.shape[0] // depth

    def load(i):
        return pltpu.make_async_copy(
            w_in_hbm.at[pl.ds(i * depth, depth)], raw.at[i % 2], raw_sem.at[i % 2]
        )

    load_out = pltpu.make_async_copy(w_out_hbm, w_out, w_sem.at[0])
    load(0).start()
    load(1).start()
    load_out.start()

    def split(i):
        load(i).wait()
        some = 64

        def step(k, carry):
            at = pl.ds(pl.multiple_of(k * some, some), some)
            to = pl.ds(pl.multiple_of(i * depth + k * some, some), some)
            w_in[to, :] = raw[i % 2, at].reshape(some, 2 * hidden)
            return carry

        lax.fori_loop(0, depth // some, step, 0)
        if i + 2 < n_loads:
            load(i + 2).start()

    barrier = pltpu.get_barrier_semaphore()
    partners = [to_z(j) for j in range(1, n_z)] + [to_x, to_y, to_sib]
    for partner in partners:
        pl.semaphore_signal(barrier, inc=1, device_id=partner, device_id_type=MESH)

    own = jnp.concatenate([tok_ref[...].astype(F32), dy_ref[...].astype(F32)], axis=0)
    for h in range(2):
        buf[expert, quarter(0, h)] = own[:, h * part : (h + 1) * part].astype(BF16)
    lanes_of = lax.broadcasted_iota(jnp.int32, (rows, 128), 1)
    experts_of = lax.broadcasted_iota(jnp.int32, (128, rows), 0)
    named, weight = routing_ref[...], gates_ref[...]
    table = jnp.zeros((128, rows), F32)
    for k in range(named.shape[0]):
        table += jnp.where(named[k : k + 1] == experts_of, weight[k : k + 1], 0.0)
    tables[expert] = table.T
    pl.semaphore_wait(barrier, len(partners))

    pending = []

    def send(src, dst, send_sem, recv_sem, target):
        copy = pltpu.make_async_remote_copy(
            src_ref=src,
            dst_ref=dst,
            send_sem=send_sem,
            recv_sem=recv_sem,
            device_id=target,
            device_id_type=MESH,
        )
        copy.start()
        pending.append(copy)
        return copy

    def pass_on(j, dx, dy, h, target, sem):
        e, q = expert_at(j, dx, core), quarter(dy, h)
        send(buf.at[e, q], buf.at[e, q], sem, g_recv.at[e, q], target)

    def arrived(j, dx, dy, h, c):
        e, q = expert_at(j, dx, c), quarter(dy, h)
        pltpu.make_async_remote_copy(
            src_ref=buf.at[e, q],
            dst_ref=buf.at[e, q],
            send_sem=gs_send.at[0],
            recv_sem=g_recv.at[e, q],
            device_id=to_sib,
            device_id_type=MESH,
        ).wait_recv()

    def to_sibling(j, dx, dy, h):
        pass_on(j, dx, dy, h, to_sib, gs_send.at[((j * 2 + dx) * 2 + dy) * 2 + h])

    def along_x(j, dy, h):
        pass_on(j, 0, dy, h, to_x, gx_send.at[(j * 2 + dy) * 2 + h])

    def along_y(j, dx, h):
        pass_on(j, dx, 0, h, to_y, gy_send.at[(j * 2 + dx) * 2 + h])

    def pass_table(j, dx, target, sem):
        e = expert_at(j, dx, core)
        send(tables.at[e], tables.at[e], sem, t_recv.at[e], target)

    def table_arrived(j, dx, c):
        e = expert_at(j, dx, c)
        pltpu.make_async_remote_copy(
            src_ref=tables.at[e],
            dst_ref=tables.at[e],
            send_sem=ts_send.at[0],
            recv_sem=t_recv.at[e],
            device_id=to_sib,
            device_id_type=MESH,
        ).wait_recv()

    def spread(j, h):
        if j:
            arrived(j, 0, 0, h, core)
        along_x(j, 0, h)
        along_y(j, 0, h)
        to_sibling(j, 0, 0, h)

    def spread_table(j):
        if j:
            table_arrived(j, 0, core)
        pass_table(j, 0, to_x, tx_send.at[j])
        pass_table(j, 0, to_sib, ts_send.at[2 * j])

    def second_a(j):
        arrived(j, 1, 0, 0, core)
        along_y(j, 1, 0)
        to_sibling(j, 1, 0, 0)

    def second_b(j):
        arrived(j, 0, 1, 1, core)
        along_x(j, 1, 1)
        to_sibling(j, 0, 1, 1)

    z_order = [1, n_z - 1] + list(range(2, n_z - 1))
    near, rest = z_order[:2], z_order[2:]
    for j in z_order:
        pass_table(0, 0, to_z(j), tz_send.at[j - 1])
    for h in range(2):
        for j in z_order:
            pass_on(0, 0, 0, h, to_z(j), gz_send.at[(j - 1) * 2 + h])
    spread(0, 0)
    spread(0, 1)
    spread_table(0)
    per = -(-n_loads // 4)

    def split_some(k):
        for i in range(k * per, min((k + 1) * per, n_loads)):
            split(i)

    split_some(0)
    for j in near:
        spread_table(j)
        spread(j, 0)
    second_a(0)
    second_b(0)
    split_some(1)
    for j in rest:
        spread_table(j)
        spread(j, 0)
    for j in near:
        second_a(j)
    split_some(2)
    for j in near:
        spread(j, 1)
    keep_scaled = []

    def forward(dy, h, first):
        q = quarter(dy, h)

        def lay(p, carry):
            at = pl.ds(pl.multiple_of(p * (2 * rows), 2 * rows), 2 * rows)
            even = buf[2 * p, q].astype(F32)
            odd = buf[2 * p + 1, q].astype(F32)
            xs[at, :] = jnp.concatenate([even[:rows], odd[:rows]], axis=0).astype(BF16)
            both = jnp.concatenate([even[rows:], odd[rows:]], axis=0)
            scaled[q, at, :] = (gate_ref[at, 0:1] * both).astype(BF16)
            return carry

        lax.fori_loop(0, n_chips, lay, 0)
        k = len(keep_scaled)
        copy = pltpu.make_async_copy(scaled.at[q], scaled_hbm.at[q], out_sem.at[k])
        copy.start()
        keep_scaled.append(copy)
        if first:
            load_out.wait()
        tile = hidden
        deep = pl.ds(pl.multiple_of(q * part, part), part)

        def gates_up(n, carry):
            at = pl.ds(pl.multiple_of(n * tile, tile), tile)
            piece = jnp.dot(xs[...], w_in[deep, at], preferred_element_type=F32)
            gate_up[:, at] = piece if first else gate_up[:, at] + piece
            return carry

        lax.fori_loop(0, 2 * hidden // tile, gates_up, 0)

        def grads(n, carry):
            at = pl.ds(pl.multiple_of(n * tile, tile), tile)
            piece = lax.dot_general(scaled[q], w_out[at, deep], NT, preferred_element_type=F32)
            act_grad[:, at] = piece if first else act_grad[:, at] + piece
            return carry

        lax.fori_loop(0, hidden // tile, grads, 0)

    def from_sibling(dy, h):
        for j in range(n_z):
            for dx in range(2):
                arrived(j, dx, dy, h, other)

    def third(dy, h, dxs):
        for j in [0] + z_order:
            for dx in dxs:
                arrived(j, dx, dy, h, core)
                to_sibling(j, dx, dy, h)

    for j in rest:
        second_a(j)
    for j in range(n_z):
        table_arrived(j, 1, core)
        pass_table(j, 1, to_sib, ts_send.at[2 * j + 1])
    split_some(3)
    for j in range(n_z):
        for dx in range(2):
            table_arrived(j, dx, other)
    for e in range(2 * n_chips):
        mine = jnp.sum(jnp.where(lanes_of == expert, tables[e], 0.0), axis=1, keepdims=True)
        gate_ref[e * rows : (e + 1) * rows, :] = jnp.broadcast_to(mine, (rows, 128))
    from_sibling(0, 0)
    forward(0, 0, True)
    for j in rest:
        spread(j, 1)
    for j in z_order:
        second_b(j)
    third(0, 1, [1])
    from_sibling(0, 1)
    forward(0, 1, False)
    third(1, 0, [0, 1])
    third(1, 1, [1])
    from_sibling(1, 0)
    forward(1, 0, False)
    from_sibling(1, 1)
    forward(1, 1, False)

    def middle(r, carry):
        at = pl.ds(pl.multiple_of(r * (2 * rows), 2 * rows), 2 * rows)
        gate_proj = gate_up[at, :hidden]
        up_proj = gate_up[at, hidden:]
        grad = act_grad[at, :]
        sig = jax.nn.sigmoid(gate_proj)
        act[at, :] = (gate_proj * sig * up_proj).astype(BF16)
        grad_both[at, :hidden] = (grad * up_proj * sig * (1.0 + gate_proj * (1.0 - sig))).astype(BF16)
        grad_both[at, hidden:] = (grad * gate_proj * sig).astype(BF16)
        return carry

    lax.fori_loop(0, n_chips, middle, 0)

    def backward(dy, h, part_at):
        q = quarter(dy, h)
        tile = part // 2

        lanes = pl.ds(part_at * tile, tile)
        at = pl.ds(pl.multiple_of(q * part + part_at * tile, tile), tile)
        out = jnp.dot(act[...], w_out[:, at], preferred_element_type=F32) * gate_ref[:, 0:1]
        back = lax.dot_general(grad_both[...], w_in[at, :], NT, preferred_element_type=F32)
        for e in range(2 * n_chips):
            take = slice(e * rows, (e + 1) * rows)
            parts[e % 2, q, e // 2, :, lanes] = jnp.concatenate(
                [out[take], back[take]], axis=0
            ).astype(BF16)
        sib_copies[dy, h, part_at] = send(
            parts.at[other, q, :, :, lanes],
            sib_in.at[q, :, :, lanes],
            s_send.at[q, part_at],
            s_recv.at[q, part_at],
            to_sib,
        )

    def half(part_at):
        return pl.ds(part_at * (part // 2), part // 2)

    def chip_sum(dy, h, part_at):
        q = quarter(dy, h)
        lanes = half(part_at)
        sib_copies[dy, h, part_at].wait_recv()

        def add(p, carry):
            parts[core, q, p, :, lanes] = (
                parts[core, q, p, :, lanes].astype(F32) + sib_in[q, p, :, lanes].astype(F32)
            ).astype(BF16)
            return carry

        lax.fori_loop(0, n_chips, add, 0)

    def first_a(j, dx, part_at):
        k, lanes = j * 2 + dx, half(part_at)
        return send(
            parts.at[core, quarter(1, 0), chip_at(j, dx), :, lanes],
            one_a.at[k, :, lanes],
            one_send.at[k, part_at],
            one_a_recv.at[k, part_at],
            to_y,
        )

    def first_b(j, dy, part_at):
        k, lanes = j * 2 + dy, half(part_at)
        return send(
            parts.at[core, quarter(dy, 1), chip_at(j, 1), :, lanes],
            one_b.at[k, :, lanes],
            one_send.at[2 * n_z + k, part_at],
            one_b_recv.at[k, part_at],
            to_x,
        )

    far = [1 + k for k in range(n_z - 1)] + [0]
    a_copies, b_copies, sib_copies = {}, {}, {}

    def send_a(part_at):
        chip_sum(1, 0, part_at)
        for dx in (1, 0):
            for j in far:
                a_copies[j, dx, part_at] = first_a(j, dx, part_at)

    def send_b(dy, part_at):
        chip_sum(dy, 1, part_at)
        for j in far:
            b_copies[j, dy, part_at] = first_b(j, dy, part_at)

    backward(1, 0, 0)
    backward(1, 1, 0)
    send_a(0)
    backward(1, 0, 1)
    send_b(1, 0)
    backward(1, 1, 1)
    send_a(1)
    backward(0, 1, 0)
    send_b(1, 1)
    backward(0, 1, 1)
    send_b(0, 0)
    backward(0, 0, 0)
    send_b(0, 1)
    backward(0, 0, 1)
    chip_sum(0, 0, 0)
    chip_sum(0, 0, 1)

    keep_act = pltpu.make_async_copy(act_t, act_t_hbm, w_sem.at[1])
    two_copies = {}
    for k, j in enumerate(far):
        if k == len(far) - 1:
            act_t[...] = act[...].T
            keep_act.start()
        p = chip_at(j, 1)
        qa, qb = quarter(0, 0), quarter(1, 1)
        for i in range(2):
            a_copies[j, 1, i].wait_recv()
        parts[core, qa, p] = (
            parts[core, qa, p].astype(F32) + one_a[j * 2 + 1].astype(F32)
        ).astype(BF16)
        two_copies[j, 0] = send(
            parts.at[core, qa, p], two.at[0, j], two_send.at[0, j], two_recv.at[0, j], to_x
        )
        p = chip_at(j, 0)
        for i in range(2):
            b_copies[j, 1, i].wait_recv()
        parts[core, qb, p] = (
            parts[core, qb, p].astype(F32) + one_b[j * 2 + 1].astype(F32)
        ).astype(BF16)
        two_copies[j, 1] = send(
            parts.at[core, qb, p], two.at[1, j], two_send.at[1, j], two_recv.at[1, j], to_y
        )

    three_copies = {}
    for j in far:
        for h in range(2):
            q, p = quarter(0, h), chip_at(j, 0)
            first = (a_copies, b_copies)[h]
            held = (one_a, one_b)[h]
            for i in range(2):
                first[j, 0, i].wait_recv()
            two_copies[j, h].wait_recv()
            total = (
                parts[core, q, p].astype(F32)
                + held[j * 2].astype(F32)
                + two[h, j].astype(F32)
            )
            if j:
                parts[core, q, p] = total.astype(BF16)
                three_copies[j, h] = send(
                    parts.at[core, q, p],
                    three.at[h, j - 1],
                    three_send.at[h, j - 1],
                    three_recv.at[h, j - 1],
                    to_z(j),
                )
            else:
                for i in range(1, n_z):
                    three_copies[i, h].wait_recv()
                    total = total + three[h, i - 1].astype(F32)
                lanes = slice(h * part, (h + 1) * part)
                mixed_ref[:, lanes] = total[:rows].astype(BF16)
                gtok_ref[:, lanes] = total[rows:].astype(BF16)

    for copy in pending:
        copy.wait_send()
    for copy in keep_scaled:
        copy.wait()
    keep_act.wait()


def last_kernel(act_t_ref, scaled_ref, mixed_in, gtok_in, mixed_ref, gtok_ref, gdown_ref):
    @pl.when(pl.program_id(0) == 0)
    def _():
        mixed_ref[...] = mixed_in[...]
        gtok_ref[...] = gtok_in[...]

    gdown_ref[...] = jnp.dot(act_t_ref[...], scaled_ref[0], preferred_element_type=F32).astype(BF16)


def dense(tokens, grad_out, routing, gates, w_in, w_out):
    n_experts = lax.axis_size("expert")
    n_z = n_experts // 4
    rows, width = tokens.shape
    part = width // 2
    model_width, hidden = w_out.shape[2], w_out.shape[1]
    slots = n_experts * rows
    vmem = pl.BlockSpec(memory_space=pltpu.VMEM)
    anywhere = pl.BlockSpec(memory_space=pl.ANY)
    block = (2 * rows, part)
    dma = pltpu.SemaphoreType.DMA
    flops = 2 * slots * model_width * hidden * 7
    depth = max(model_width // 8, 64)
    mixed, gtok, act_t, scaled = pl.pallas_call(
        functools.partial(fused_kernel, n_z),
        out_shape=(
            jax.ShapeDtypeStruct((rows, width), BF16),
            jax.ShapeDtypeStruct((rows, width), BF16),
            jax.ShapeDtypeStruct((hidden, slots), BF16),
            jax.ShapeDtypeStruct((4, slots, part), BF16),
        ),
        in_specs=[vmem, vmem, vmem, vmem, anywhere, anywhere],
        out_specs=(vmem, vmem, anywhere, anywhere),
        scratch_shapes=[
            pltpu.VMEM((n_experts, rows, 128), F32),
            pltpu.VMEM((slots, 128), F32),
            pltpu.VMEM((2, depth, 2, hidden), BF16),
            pltpu.VMEM((n_experts, 4) + block, BF16),
            pltpu.VMEM((2, 4, 2 * n_z) + block, BF16),
            pltpu.VMEM((4, 2 * n_z) + block, BF16),
            pltpu.VMEM((2 * n_z,) + block, BF16),
            pltpu.VMEM((2 * n_z,) + block, BF16),
            pltpu.VMEM((2, n_z) + block, BF16),
            pltpu.VMEM((2, n_z - 1) + block, BF16),
            pltpu.VMEM((slots, part), BF16),
            pltpu.VMEM((4, slots, part), BF16),
            pltpu.VMEM((slots, 2 * hidden), F32),
            pltpu.VMEM((slots, hidden), F32),
            pltpu.VMEM((slots, hidden), BF16),
            pltpu.VMEM((hidden, slots), BF16),
            pltpu.VMEM((slots, 2 * hidden), BF16),
            pltpu.VMEM((model_width, 2 * hidden), BF16),
            pltpu.VMEM((hidden, model_width), BF16),
            dma((2,)),
            dma((2,)),
            dma((n_z - 1,)),
            dma((n_z,)),
            dma((2 * n_z,)),
            dma((n_experts,)),
            dma((2 * (n_z - 1),)),
            dma((4 * n_z,)),
            dma((4 * n_z,)),
            dma((8 * n_z,)),
            dma((n_experts, 4)),
            dma((4, 2)),
            dma((4, 2)),
            dma((4 * n_z, 2)),
            dma((2 * n_z, 2)),
            dma((2 * n_z, 2)),
            dma((2, n_z)),
            dma((2, n_z)),
            dma((2, n_z - 1)),
            dma((2, n_z - 1)),
            dma((4,)),
        ],
        compiler_params=pltpu.CompilerParams(
            collective_id=0, has_side_effects=True, vmem_limit_bytes=60 * 1024 * 1024
        ),
        cost_estimate=pl.CostEstimate(
            flops=flops, bytes_accessed=8 * model_width * hidden, transcendentals=slots * hidden
        ),
    )(tokens, grad_out, routing.T, gates.T, w_in[0], w_out[0])
    tile = part // 2
    whole = pl.BlockSpec((rows, width), lambda n: (0, 0))
    mixed, gtok, gdown = pl.pallas_call(
        last_kernel,
        grid=(8,),
        out_shape=(
            jax.ShapeDtypeStruct((rows, width), BF16),
            jax.ShapeDtypeStruct((rows, width), BF16),
            jax.ShapeDtypeStruct((hidden, model_width), BF16),
        ),
        in_specs=[
            pl.BlockSpec((hidden, slots), lambda n: (0, 0)),
            pl.BlockSpec((1, slots, tile), lambda n: (n // 2, 0, n % 2)),
            whole,
            whole,
        ],
        out_specs=(whole, whole, pl.BlockSpec((hidden, tile), lambda n: (0, n))),
        compiler_params=pltpu.CompilerParams(vmem_limit_bytes=60 * 1024 * 1024),
        cost_estimate=pl.CostEstimate(
            flops=flops // 7, bytes_accessed=4 * model_width * hidden, transcendentals=0
        ),
    )(act_t, scaled, mixed, gtok)
    return mixed, gtok, gdown[None]


def shards(tokens, grad_out, routing, gates, w_in, w_out):
    n_experts = lax.axis_size("expert")
    rows = tokens.shape[0]
    whole_groups = 16 * rows // n_experts >= rows
    if whole_groups and n_experts % 4 == 0 and n_experts >= 16 and lax.axis_size("tensor") == 2:
        return dense(tokens, grad_out, routing, gates, w_in, w_out)
    return dispatched(tokens, grad_out, routing, gates, w_in, w_out)


def solution(mesh):
    in_specs = (
        P("expert", "tensor"),
        P("expert", "tensor"),
        P("expert", None),
        P("expert", None),
        P("expert", None, None, "tensor"),
        P("expert", "tensor", None),
    )
    out_specs = (P("expert", "tensor"), P("expert", "tensor"), P("expert", "tensor", None))
    return jax.shard_map(shards, mesh=mesh, in_specs=in_specs, out_specs=out_specs, check_vma=False)
```
